256 devices in a mesh: ctx: 8 (over x_lo, y), head: 32 (over x_hi, z, core).
Axes of the slice: x: 4 (x_hi: 2, x_lo: 2; x = x_hi * 2 + x_lo), y: 4, z: 8, core: 2. Of those that a mesh axis runs over, the one named last changes fastest.
Arguments:
- tokens: bfloat16 [4096, 4096], P('ctx', 'head'), may hold values from -6 to 6
- lengths: int32 [64], replicated, may hold values from 1 to 512, 4096 in all
- gain_one: float32 [4096], replicated, may hold values from 0.1 to 1.9
- qkv_one: bfloat16 [4096, 3, 4096], P(None, None, 'head')
- out_one: bfloat16 [4096, 4096], P('head'), may hold values from -0.5 to 0.5
- gain_two: float32 [4096], replicated, may hold values from 0.1 to 1.9
- qkv_two: bfloat16 [4096, 3, 4096], P(None, None, 'head')
- out_two: bfloat16 [4096, 4096], P('head'), may hold values from -0.5 to 0.5
Outputs:
- stream_out: bfloat16 [4096, 4096], P('ctx', 'head')
The draws below stay inside these ranges and needn't reach their ends.
Inputs may be any that keep to these rules, and one draw needn't show every extreme that they name: The lengths sum to 4096; the longest is exactly 512.
All inputs are finite; a program needn't handle non-finite values.
Results may differ from the reference program's by a relative error of at most 0.0085.
Values may be sent and summed in bfloat16 or wider, within the bound.
No kernel may reach another device: no remote copies, remote signals or barrier semaphores. Data moves between devices by JAX's collectives and lax.ppermute only.
A program may use at most 128 MiB of HBM per device.

```python
import math
import jax
import jax.numpy as jnp
import numpy as np
from jax import lax

D = 4096
HD = 128
HEADS = 32
TOKENS = 4096
SEQS = 64
MOST = 512


def base_weights(key, salt):
    base = jax.random.normal(jax.random.fold_in(key, salt), (D, 3, HEADS * HD), jnp.float32)
    return jnp.clip(base, -6.0, 6.0) * D ** (-0.5)


def draw_tokens(key, part):
    noise = jax.random.normal(jax.random.fold_in(key, 11), (TOKENS, D), jnp.float32)
    rows = noise
    return jnp.clip(rows, -6.0, 6.0).astype(jnp.bfloat16)


def draw_qkv_one(key, part):
    weights = base_weights(key, 101)
    return weights.astype(jnp.bfloat16)


def draw_qkv_two(key, part):
    weights = base_weights(key, 201)
    return weights.astype(jnp.bfloat16)


def levels(stream_key, dims, pieces, least, largest):
    factor_of = 1.0
    for dim, blocks in pieces:
        heights = jax.random.uniform(jax.random.fold_in(jax.random.fold_in(stream_key, 6), dim), (blocks,), jnp.float32, least / len(pieces), largest / len(pieces))
        factor_of = factor_of * jnp.repeat(jnp.exp(heights), dims[dim] // blocks).reshape((-1,) + (1,) * (len(dims) - 1 - dim))
    return factor_of


def length_profile(count, total, most, skew):
    weights = [(1 << 20) // math.isqrt(standing ** skew) + 1 for standing in range(2, count + 1)]
    spare, given = total - most - (count - 1), [1] * (count - 1)
    while spare > 0:
        movable = [i for i in range(count - 1) if given[i] < most]
        whole, left = sum([weights[i] for i in movable]), spare
        for i in movable:
            more = min(most - given[i], max(1, left * weights[i] // whole), spare)
            given[i] = given[i] + more
            spare = spare - more
    return np.array([most] + given)


def ragged(rng, count, total, most, lean):
    if count == 2:
        one = jax.random.randint(rng, (), max(1, total - most), min(most, total - 1) + 1)
        return jnp.stack([one, total - one])
    tallies = jnp.asarray(length_profile(count, total, most, lean), jnp.int32)
    couples = (count - 1) // 2
    source_of, receiver = tallies[1:1 + 2 * couples:2], tallies[2:2 + 2 * couples:2]
    room = jnp.minimum(source_of - 1, most - receiver)
    passed = jax.random.randint(jax.random.fold_in(rng, 1), (couples,), 0, 1 << 20) % (room + 1)
    tallies = tallies.at[1:1 + 2 * couples:2].set(source_of - passed).at[2:2 + 2 * couples:2].set(receiver + passed)
    return tallies[jax.random.permutation(jax.random.fold_in(rng, 2), count)]


def gaussian(own_key, shape, scale, bound, pieces=(), kind=jnp.bfloat16):
    values = scale * jax.random.normal(own_key, shape, jnp.float32)
    if pieces:
        values = values * levels(own_key, shape, pieces, -0.22, 0.18)
    return jnp.clip(values, -bound, bound).astype(kind)


def setup_inputs(seed: int = 0) -> dict:
    key_list = jax.random.split(jax.random.key(seed), 9)
    tokens = draw_tokens(jax.random.fold_in(key_list[8], 71), 0)
    lengths = ragged(key_list[1], SEQS, TOKENS, MOST, 2).astype(jnp.int32)
    gain_one = jnp.clip(1.0 + 0.18 * jax.random.normal(key_list[2], (D,), jnp.float32), 0.1, 1.9)
    qkv_one = draw_qkv_one(jax.random.fold_in(key_list[8], 71), 0)
    out_one = gaussian(key_list[4], (HEADS * HD, D), HD ** -0.5, 0.5, ((0, 32),))
    gain_two = jnp.clip(1.0 + 0.18 * jax.random.normal(key_list[5], (D,), jnp.float32), 0.1, 1.9)
    qkv_two = draw_qkv_two(jax.random.fold_in(key_list[8], 71), 0)
    out_two = gaussian(key_list[7], (HEADS * HD, D), HD ** -0.5, 0.5, ((0, 32),))
    return dict(tokens=tokens, lengths=lengths, gain_one=gain_one, qkv_one=qkv_one, out_one=out_one, gain_two=gain_two, qkv_two=qkv_two, out_two=out_two)


EPS = 1e-05

def norm_rows(rows, gain):
    wide = rows.astype(jnp.float32)
    factor = lax.rsqrt(lax.optimization_barrier(jnp.mean(wide * wide, axis=-1, keepdims=True)) + EPS)
    return (wide * factor * gain.astype(jnp.float32)).astype(jnp.bfloat16)

def head_attend(query, keys, values, allowed):
    scores = jnp.dot(query, keys.T, preferred_element_type=jnp.float32) * HD ** (-0.5)
    scores = jnp.where(allowed, scores, -1e+30)
    top = lax.optimization_barrier(jnp.max(scores, axis=1, keepdims=True))
    expo = jnp.where(allowed, jnp.exp(scores - top), 0.0)
    total = lax.optimization_barrier(jnp.sum(expo, axis=1, keepdims=True))
    weights = expo.astype(jnp.bfloat16)
    return (jnp.dot(weights, values, preferred_element_type=jnp.float32) / total).astype(jnp.bfloat16)

def sublayer(stream, gain, wqkv, wout, allowed):
    normed = norm_rows(stream, gain)
    proj = jnp.dot(normed, wqkv.reshape(D, 3 * HEADS * HD), preferred_element_type=jnp.float32)
    proj = proj.astype(jnp.bfloat16).reshape(TOKENS, 3, HEADS, HD)
    per_head = jnp.transpose(proj, (2, 1, 0, 3))
    outputs = lax.map(lambda item: head_attend(item[0], item[1], item[2], allowed), per_head)
    attn = jnp.transpose(outputs, (1, 0, 2)).reshape(TOKENS, HEADS * HD)
    mixed = jnp.dot(attn, wout, preferred_element_type=jnp.float32)
    return (stream.astype(jnp.float32) + mixed).astype(jnp.bfloat16)

def reference(tokens, lengths, gain_one, qkv_one, out_one, gain_two, qkv_two, out_two):
    position = jnp.arange(TOKENS, dtype=jnp.int32)
    ends = jnp.cumsum(lengths).astype(jnp.int32)
    seg = lax.optimization_barrier(jnp.sum((ends[None, :] <= position[:, None]).astype(jnp.int32), axis=1))
    causal = position[None, :] <= position[:, None]
    within = causal & (seg[None, :] == seg[:, None])
    stream_one = sublayer(tokens, gain_one, qkv_one, out_one, within)
    return sublayer(stream_one, gain_two, qkv_two, out_two, causal)
```

```python
import jax
import jax.numpy as jnp
from jax import lax
from jax.experimental import pallas as pl
from jax.experimental.pallas import tpu as pltpu
from jax.sharding import PartitionSpec as P

HD = 128
EPS = 1e-05
D = 4096
ROWS = 512
Z = 8
SCALE = HD ** (-0.5)
STEPS = (0, -1, 1, -2, 2, -3, 3, 4)
ANYWHERE = pl.BlockSpec(memory_space=pltpu.VMEM)
SCALARS = pl.BlockSpec(memory_space=pltpu.SMEM)


def call(kernel, out, *args, flops=0, moved=0, scratch=()):
    return pl.pallas_call(
        kernel,
        out_shape=out,
        in_specs=[SCALARS] + [ANYWHERE] * (len(args) - 1),
        out_specs=jax.tree.map(lambda _: ANYWHERE, out),
        scratch_shapes=list(scratch),
        compiler_params=pltpu.CompilerParams(vmem_limit_bytes=40 * 2**20),
        cost_estimate=pl.CostEstimate(flops=flops, bytes_accessed=moved, transcendentals=0),
    )(*args)


def head_perm(dxh=0, dz=0, dc=0):
    pairs = []
    for xh in range(2):
        for z in range(Z):
            for c in range(2):
                to = ((xh + dxh) % 2) * 16 + ((z + dz) % Z) * 2 + (c + dc) % 2
                pairs.append((xh * 16 + z * 2 + c, to))
    return pairs


def ctx_perm(dxl=0, dy=0):
    return [
        (xl * 4 + y, ((xl + dxl) % 2) * 4 + (y + dy) % 4) for xl in range(2) for y in range(4)
    ]


def along_z(value, steps):
    return lax.ppermute(value, "head", head_perm(dz=steps))


def to_other_core(value):
    return lax.ppermute(value, "head", head_perm(dc=1))


def gather_half(block):
    with jax.named_scope("gather_half"):
        other = lax.ppermute(block, "head", head_perm(dxh=1))
        pair = jnp.concatenate([block, other], axis=0)
        f1, b1, f2, b2 = (along_z(pair, k) for k in (1, -1, 2, -2))
        f3, b3 = along_z(f2, 1), along_z(b2, -1)
        g1, g2 = along_z(f2[:ROWS], 2), along_z(b2[ROWS:], -2)
        return (pair, f1, b1, f2, b2, f3, b3, g1, g2)


def pieces(refs):
    for ref in refs[:7]:
        yield ref[:ROWS, :], ref[ROWS:, :]
    yield refs[7][...], refs[8][...]


def project_kernel(where, *refs):
    blocks, (gain, mine, others, out_ref, send_ref) = refs[:9], refs[9:]
    xh, z, c = where[0], where[1], where[2]
    acc = jnp.zeros((ROWS, 768), jnp.float32)
    squares = jnp.zeros((ROWS, HD), jnp.float32)
    for step, (one, two) in zip(STEPS, pieces(blocks)):
        at = jnp.bitwise_and(z + step, Z - 1)
        scaled, weights = [], []
        for rows, x in ((one, xh), (two, 1 - xh)):
            wide = rows.astype(jnp.float32)
            squares += wide * wide
            chip = x * Z + at
            head = chip * 2 + c
            scaled.append((wide * gain[pl.ds(head, 1), :]).astype(jnp.bfloat16))
            first = pl.multiple_of(head * HD, HD)
            half = pl.multiple_of(chip * HD, HD)
            weights.append(
                jnp.concatenate(
                    [mine[t, pl.ds(first, HD), :] for t in range(3)]
                    + [others[t, pl.ds(half, HD), :] for t in range(3)],
                    axis=1,
                )
            )
        acc += jnp.dot(
            jnp.concatenate(scaled, axis=1),
            jnp.concatenate(weights, axis=0),
            preferred_element_type=jnp.float32,
        )
    total = jnp.broadcast_to(jnp.sum(squares, axis=1, keepdims=True), (ROWS, HD))
    out_ref[:, :384] = acc[:, :384]
    out_ref[:, 384:] = total
    send_ref[:, :384] = acc[:, 384:]
    send_ref[:, 384:] = total


def finish_kernel(where, own, came, q_ref, kv_ref):
    total = own[:, 384:] + came[:, 384:]
    factor = lax.rsqrt(total * (1.0 / D) + EPS)
    q_ref[...] = ((own[:, :128] + came[:, :128]) * factor).astype(jnp.bfloat16)
    kv_ref[:, :128] = ((own[:, 128:256] + came[:, 128:256]) * factor).astype(jnp.bfloat16)
    kv_ref[:, 128:] = ((own[:, 256:384] + came[:, 256:384]) * factor).astype(jnp.bfloat16)


def project(where, block, gain, mine, others):
    blocks = gather_half(block)
    with jax.named_scope("project"):
        wide = jax.ShapeDtypeStruct((ROWS, 512), jnp.float32)
        own, send = call(
            project_kernel,
            (wide, wide),
            where,
            *blocks,
            gain.reshape(32, HD),
            mine,
            others,
            flops=2 * ROWS * 2048 * 768,
            moved=8 * 2**20,
        )
        came = to_other_core(send)
        return call(
            finish_kernel,
            (
                jax.ShapeDtypeStruct((ROWS, HD), jnp.bfloat16),
                jax.ShapeDtypeStruct((ROWS, 2 * HD), jnp.bfloat16),
            ),
            where,
            own,
            came,
            moved=3 * 2**20,
        )


def scores_of(query, keys):
    return (
        lax.dot_general(query, keys, (((1,), (1,)), ((), ())), preferred_element_type=jnp.float32)
        * SCALE
    )


def within_kernel(where, starts, q_ref, kv_ref, prev_ref, out_ref):
    query = q_ref[...]
    first = where[5] * ROWS
    start = starts[...]
    row = lax.broadcasted_iota(jnp.int32, (ROWS, ROWS), 0) + first
    col = lax.broadcasted_iota(jnp.int32, (ROWS, ROWS), 1) + first
    ok_own = (col <= row) & (col >= start)
    ok_prev = (col - ROWS) >= start
    s_own = jnp.where(ok_own, scores_of(query, kv_ref[:, :HD]), -1e30)
    s_prev = jnp.where(ok_prev, scores_of(query, prev_ref[:, :HD]), -1e30)
    top = jnp.maximum(
        jnp.max(s_own, axis=1, keepdims=True), jnp.max(s_prev, axis=1, keepdims=True)
    )
    e_own = jnp.exp(s_own - top)
    e_prev = jnp.exp(s_prev - top)
    total = jnp.sum(e_own, axis=1, keepdims=True) + jnp.sum(e_prev, axis=1, keepdims=True)
    mixed = jnp.dot(
        e_own.astype(jnp.bfloat16), kv_ref[:, HD:], preferred_element_type=jnp.float32
    ) + jnp.dot(e_prev.astype(jnp.bfloat16), prev_ref[:, HD:], preferred_element_type=jnp.float32)
    out_ref[...] = (mixed / total).astype(jnp.bfloat16)


def across_kernel(where, q_ref, kv0, kv1, kv2, kv3, out_ref, top_s, total_s, mixed_s):
    xl, y, index = where[3], where[4], where[5]
    query = q_ref[...]
    s = scores_of(query, kv0[:ROWS, :HD])
    row = lax.broadcasted_iota(jnp.int32, (ROWS, ROWS), 0)
    col = lax.broadcasted_iota(jnp.int32, (ROWS, ROWS), 1)
    s = jnp.where(col <= row, s, -1e30)
    top = jnp.max(s, axis=1, keepdims=True)
    expo = jnp.exp(s - top)
    top_s[...] = top
    total_s[...] = jnp.sum(expo, axis=1, keepdims=True)
    mixed_s[...] = jnp.dot(
        expo.astype(jnp.bfloat16), kv0[:ROWS, HD:], preferred_element_type=jnp.float32
    )
    for ref, dy in ((kv0, 0), (kv1, -1), (kv2, 1), (kv3, 2)):
        for part in range(2):
            if dy == 0 and part == 0:
                continue
            owner = (xl if part == 0 else 1 - xl) * 4 + jnp.bitwise_and(y + dy, 3)

            @pl.when(owner < index)
            def _(ref=ref, part=part):
                rows = pl.ds(part * ROWS, ROWS)
                s = scores_of(query, ref[rows, :HD])
                old = top_s[...]
                top = jnp.maximum(old, jnp.max(s, axis=1, keepdims=True))
                expo = jnp.exp(s - top)
                shrink = jnp.exp(old - top)
                top_s[...] = top
                total_s[...] = total_s[...] * shrink + jnp.sum(expo, axis=1, keepdims=True)
                mixed_s[...] = mixed_s[...] * shrink + jnp.dot(
                    expo.astype(jnp.bfloat16), ref[rows, HD:], preferred_element_type=jnp.float32
                )

    out_ref[...] = (mixed_s[...] / total_s[...]).astype(jnp.bfloat16)


def mix_kernel(where, *refs):
    blocks, (weights, out_ref, send_ref) = refs[:9], refs[9:]
    xh, z, c = where[0], where[1], where[2]
    acc = jnp.zeros((ROWS, 256), jnp.float32)
    for step, (one, two) in zip(STEPS, pieces(blocks)):
        at = jnp.bitwise_and(z + step, Z - 1)
        rows = [
            weights[pl.ds(pl.multiple_of((x * Z + at) * HD, HD), HD), :] for x in (xh, 1 - xh)
        ]
        acc += jnp.dot(
            jnp.concatenate([one, two], axis=1),
            jnp.concatenate(rows, axis=0),
            preferred_element_type=jnp.float32,
        )
    first = c == 0
    out_ref[...] = jnp.where(first, acc[:, :HD], acc[:, HD:])
    send_ref[...] = jnp.where(first, acc[:, HD:], acc[:, :HD])


def out_project(where, attn, weights, resid):
    blocks = gather_half(attn)
    with jax.named_scope("mix"):
        part = jax.ShapeDtypeStruct((ROWS, HD), jnp.float32)
        own, send = call(
            mix_kernel,
            (part, part),
            where,
            *blocks,
            weights,
            flops=2 * ROWS * 2048 * 256,
            moved=4 * 2**20,
        )
        came = to_other_core(send)
        return (resid.astype(jnp.float32) + (own + came)).astype(jnp.bfloat16)


def columns_of(out_one, out_two, index):
    with jax.named_scope("columns"):
        both = jnp.stack([out_one, out_two])
        part = lax.dynamic_slice_in_dim(both, index * 16, 16, axis=1)
        part = jnp.transpose(part.reshape(2, 16, 16, 256), (2, 0, 1, 3))
        groups = [[chip * 2 + c for chip in range(16)] for c in range(2)]
        part = lax.all_to_all(
            part.reshape(16, 32, 256), "head", 0, 0, axis_index_groups=groups, tiled=True
        )
        part = part.reshape(16, 2, 16, 256)
        return [
            lax.all_gather(part[:, m], "ctx", axis=1, tiled=True).reshape(2048, 256)
            for m in range(2)
        ]


def other_weights(planes, c):
    with jax.named_scope("swap"):
        split = planes.reshape(3, 16, 2, HD, HD)
        send = lax.dynamic_index_in_dim(split, 1 - c, axis=2, keepdims=False)
        return to_other_core(send.reshape(3, 2048, HD))


def local(tokens, lengths, gain_one, qkv_one, out_one, gain_two, qkv_two, out_two):
    index = lax.axis_index("ctx").astype(jnp.int32)
    head = lax.axis_index("head").astype(jnp.int32)
    c = head % 2
    where = jnp.stack([head // 16, (head // 2) % Z, c, index // 4, index % 4, index])

    planes_one = jnp.transpose(qkv_one, (1, 0, 2))
    planes_two = jnp.transpose(qkv_two, (1, 0, 2))
    others_one = other_weights(planes_one, c)
    columns_one, columns_two = columns_of(out_one, out_two, index)
    others_two = other_weights(planes_two, c)

    order = jnp.arange(lengths.shape[0])
    ends = jnp.sum(jnp.where(order[None, :] <= order[:, None], lengths[None, :], 0), axis=1)
    own_pos = index * ROWS + jnp.arange(ROWS, dtype=jnp.int32)
    starts = jnp.max(
        jnp.where(ends[None, :] <= own_pos[:, None], ends[None, :], 0), axis=1, keepdims=True
    )

    half = jax.ShapeDtypeStruct((ROWS, HD), jnp.bfloat16)
    query, kv = project(where, tokens, gain_one, planes_one, others_one)
    with jax.named_scope("within"):
        prev = lax.ppermute(kv, "ctx", [(i, i + 1) for i in range(7)])
        attn = call(within_kernel, half, where, starts, query, kv, prev, flops=2**28, moved=2**20)
    stream = out_project(where, attn, columns_one, tokens)

    query, kv = project(where, stream, gain_two, planes_two, others_two)
    with jax.named_scope("across"):
        pair = jnp.concatenate([kv, lax.ppermute(kv, "ctx", ctx_perm(dxl=1))], axis=0)
        sent = [lax.ppermute(pair, "ctx", ctx_perm(dy=k)) for k in (1, -1, 2)]
        attn = call(
            across_kernel,
            half,
            where,
            query,
            pair,
            *sent,
            flops=2**30,
            moved=2**22,
            scratch=(
                pltpu.VMEM((ROWS, 1), jnp.float32),
                pltpu.VMEM((ROWS, 1), jnp.float32),
                pltpu.VMEM((ROWS, HD), jnp.float32),
            ),
        )
    return out_project(where, attn, columns_two, stream)


def solution(mesh):
    placed = (
        P("ctx", "head"),
        P(),
        P(),
        P(None, None, "head"),
        P("head", None),
        P(),
        P(None, None, "head"),
        P("head", None),
    )
    return jax.shard_map(
        local, mesh=mesh, in_specs=placed, out_specs=P("ctx", "head"), check_vma=False
    )
```

```python
import jax
import jax.numpy as jnp
from jax import lax
from jax.experimental import pallas as pl
from jax.experimental.pallas import tpu as pltpu
from jax.sharding import PartitionSpec as P

HD = 128
EPS = 1e-05
D = 4096
ROWS = 512
Z = 8
SCALE = HD ** (-0.5)
STEPS = (0, -1, 1, -2, 2, -3, 3, 4)
ANYWHERE = pl.BlockSpec(memory_space=pltpu.VMEM)
SCALARS = pl.BlockSpec(memory_space=pltpu.SMEM)


def call(kernel, out, *args, flops=0, moved=0, scratch=()):
    return pl.pallas_call(
        kernel,
        out_shape=out,
        in_specs=[SCALARS] + [ANYWHERE] * (len(args) - 1),
        out_specs=jax.tree.map(lambda _: ANYWHERE, out),
        scratch_shapes=list(scratch),
        compiler_params=pltpu.CompilerParams(vmem_limit_bytes=40 * 2**20),
        cost_estimate=pl.CostEstimate(flops=flops, bytes_accessed=moved, transcendentals=0),
    )(*args)


def head_perm(dxh=0, dz=0, dc=0):
    pairs = []
    for xh in range(2):
        for z in range(Z):
            for c in range(2):
                to = ((xh + dxh) % 2) * 16 + ((z + dz) % Z) * 2 + (c + dc) % 2
                pairs.append((xh * 16 + z * 2 + c, to))
    return pairs


def ctx_perm(dxl=0, dy=0):
    return [
        (xl * 4 + y, ((xl + dxl) % 2) * 4 + (y + dy) % 4) for xl in range(2) for y in range(4)
    ]


def along_z(value, steps):
    return lax.ppermute(value, "head", head_perm(dz=steps))


def to_other_core(value):
    return lax.ppermute(value, "head", head_perm(dc=1))


def along_z_all(block):
    half = block.shape[0] // 2
    f1, b1, f2, b2 = (along_z(block, k) for k in (1, -1, 2, -2))
    f3, b3 = along_z(f2, 1), along_z(b2, -1)
    g1, g2 = along_z(f2[:half], 2), along_z(b2[half:], -2)
    return (block, f1, b1, f2, b2, f3, b3, g1, g2)


def over_x(value):
    return lax.ppermute(value, "head", head_perm(dxh=1))


def after(value, *others):
    return lax.optimization_barrier((value, others))[0]


def pieces(refs):
    for ref in refs[:7]:
        yield ref[:ROWS, :], ref[ROWS:, :]
    yield refs[7][...], refs[8][...]


def project_kernel(where, *refs):
    blocks, (gain, mine, others, out_ref, send_ref) = refs[:9], refs[9:]
    xh, z, c = where[0], where[1], where[2]
    acc = jnp.zeros((ROWS, 768), jnp.float32)
    squares = jnp.zeros((ROWS, HD), jnp.float32)
    for step, (one, two) in zip(STEPS, pieces(blocks)):
        at = jnp.bitwise_and(z + step, Z - 1)
        scaled, weights = [], []
        for rows, x in ((one, xh), (two, 1 - xh)):
            wide = rows.astype(jnp.float32)
            squares += wide * wide
            chip = x * Z + at
            head = chip * 2 + c
            scaled.append((wide * gain[pl.ds(head, 1), :]).astype(jnp.bfloat16))
            first = pl.multiple_of(head * HD, HD)
            half = pl.multiple_of(chip * HD, HD)
            weights.append(
                jnp.concatenate(
                    [mine[t, pl.ds(first, HD), :] for t in range(3)]
                    + [others[t, pl.ds(half, HD), :] for t in range(3)],
                    axis=1,
                )
            )
        acc += jnp.dot(
            jnp.concatenate(scaled, axis=1),
            jnp.concatenate(weights, axis=0),
            preferred_element_type=jnp.float32,
        )
    total = jnp.broadcast_to(jnp.sum(squares, axis=1, keepdims=True), (ROWS, HD))
    out_ref[:, :384] = acc[:, :384]
    out_ref[:, 384:] = total
    send_ref[:, :384] = acc[:, 384:]
    send_ref[:, 384:] = total


def finish_kernel(where, own, came, q_ref, kv_ref):
    total = own[:, 384:] + came[:, 384:]
    factor = lax.rsqrt(total * (1.0 / D) + EPS)
    q_ref[...] = ((own[:, :128] + came[:, :128]) * factor).astype(jnp.bfloat16)
    kv_ref[:, :128] = ((own[:, 128:256] + came[:, 128:256]) * factor).astype(jnp.bfloat16)
    kv_ref[:, 128:] = ((own[:, 256:384] + came[:, 256:384]) * factor).astype(jnp.bfloat16)


def project(where, blocks, gain, mine, others):
    with jax.named_scope("project"):
        wide = jax.ShapeDtypeStruct((ROWS, 512), jnp.float32)
        own, send = call(
            project_kernel,
            (wide, wide),
            where,
            *blocks,
            gain.reshape(32, HD),
            mine,
            others,
            flops=2 * ROWS * 2048 * 768,
            moved=8 * 2**20,
        )
        came = to_other_core(send)
        return call(
            finish_kernel,
            (
                jax.ShapeDtypeStruct((ROWS, HD), jnp.bfloat16),
                jax.ShapeDtypeStruct((ROWS, 2 * HD), jnp.bfloat16),
            ),
            where,
            own,
            came,
            moved=3 * 2**20,
        )


def scores_of(query, keys):
    return (
        lax.dot_general(query, keys, (((1,), (1,)), ((), ())), preferred_element_type=jnp.float32)
        * SCALE
    )


def within_kernel(where, starts, q_ref, kv_ref, prev_ref, out_ref):
    query = q_ref[...]
    first = where[5] * ROWS
    start = starts[...]
    row = lax.broadcasted_iota(jnp.int32, (ROWS, ROWS), 0) + first
    col = lax.broadcasted_iota(jnp.int32, (ROWS, ROWS), 1) + first
    ok_own = (col <= row) & (col >= start)
    ok_prev = (col - ROWS) >= start
    s_own = jnp.where(ok_own, scores_of(query, kv_ref[:, :HD]), -1e30)
    s_prev = jnp.where(ok_prev, scores_of(query, prev_ref[:, :HD]), -1e30)
    top = jnp.maximum(
        jnp.max(s_own, axis=1, keepdims=True), jnp.max(s_prev, axis=1, keepdims=True)
    )
    e_own = jnp.exp(s_own - top)
    e_prev = jnp.exp(s_prev - top)
    total = jnp.sum(e_own, axis=1, keepdims=True) + jnp.sum(e_prev, axis=1, keepdims=True)
    mixed = jnp.dot(
        e_own.astype(jnp.bfloat16), kv_ref[:, HD:], preferred_element_type=jnp.float32
    ) + jnp.dot(e_prev.astype(jnp.bfloat16), prev_ref[:, HD:], preferred_element_type=jnp.float32)
    out_ref[...] = (mixed / total).astype(jnp.bfloat16)


def start_state(query, keys, values, state):
    s = scores_of(query, keys)
    row = lax.broadcasted_iota(jnp.int32, (ROWS, ROWS), 0)
    col = lax.broadcasted_iota(jnp.int32, (ROWS, ROWS), 1)
    s = jnp.where(col <= row, s, -1e30)
    top = jnp.max(s, axis=1, keepdims=True)
    expo = jnp.exp(s - top)
    state[0][...] = top
    state[1][...] = jnp.sum(expo, axis=1, keepdims=True)
    state[2][...] = jnp.dot(expo.astype(jnp.bfloat16), values, preferred_element_type=jnp.float32)


def add_keys(query, keys, values, state):
    s = scores_of(query, keys)
    old = state[0][...]
    top = jnp.maximum(old, jnp.max(s, axis=1, keepdims=True))
    expo = jnp.exp(s - top)
    shrink = jnp.exp(old - top)
    state[0][...] = top
    state[1][...] = state[1][...] * shrink + jnp.sum(expo, axis=1, keepdims=True)
    state[2][...] = state[2][...] * shrink + jnp.dot(
        expo.astype(jnp.bfloat16), values, preferred_element_type=jnp.float32
    )


STATE = (
    pltpu.VMEM((ROWS, 1), jnp.float32),
    pltpu.VMEM((ROWS, 1), jnp.float32),
    pltpu.VMEM((ROWS, HD), jnp.float32),
)
STATS = jax.ShapeDtypeStruct((8, ROWS), jnp.float32)


def give(state, out_ref, stat_ref):
    total = state[1][...]
    out_ref[...] = (state[2][...] / total).astype(out_ref.dtype)
    lane = lax.broadcasted_iota(jnp.int32, (ROWS, HD), 1)
    both = jnp.where(lane == 0, state[0][...], total)
    stat_ref[...] = jnp.transpose(both)[:8, :]


def helped_kernel(where, q_ref, kv0, kv1, kv2, kv3, out_ref, stat_ref, *state):
    @pl.when(where[3] == 0)
    def _():
        query = q_ref[...]
        state[0][...] = jnp.full((ROWS, 1), -1e30, jnp.float32)
        state[1][...] = jnp.zeros((ROWS, 1), jnp.float32)
        state[2][...] = jnp.zeros((ROWS, HD), jnp.float32)
        for ref in (kv0, kv1, kv2, kv3):
            add_keys(query, ref[:, :HD], ref[:, HD:], state)
        give(state, out_ref, stat_ref)

    @pl.when(where[3] != 0)
    def _():
        out_ref[...] = jnp.zeros((ROWS, HD), out_ref.dtype)
        stat_ref[...] = jnp.zeros((8, ROWS), jnp.float32)


def across_kernel(where, q_ref, kv0, kv1, kv2, kv3, out_ref, stat_ref, *state):
    y = where[4]
    query = q_ref[...]
    start_state(query, kv0[:, :HD], kv0[:, HD:], state)
    for ref, dy in ((kv1, -1), (kv2, 1), (kv3, 2)):

        @pl.when(jnp.bitwise_and(y + dy, 3) < y)
        def _(ref=ref):
            add_keys(query, ref[:, :HD], ref[:, HD:], state)

    give(state, out_ref, stat_ref)


def merge_kernel(where, one, stat_one, two, stat_two, out_ref):
    a, b = stat_one[...], stat_two[...]
    second = where[3] != 0
    top_a, total_a = a[0:1, :], a[1:2, :]
    top_b = jnp.where(second, b[0:1, :], -1e30)
    total_b = jnp.where(second, b[1:2, :], 0.0)
    top = jnp.maximum(top_a, top_b)
    share_a = total_a * jnp.exp(top_a - top)
    share_b = total_b * jnp.exp(top_b - top)
    part = share_b / (share_a + share_b)
    part = jnp.transpose(jnp.broadcast_to(part, (HD, ROWS)))
    first = one[...]
    out_ref[...] = (first + (two[...].astype(jnp.float32) - first) * part).astype(jnp.bfloat16)


def across(where, query, kv):
    with jax.named_scope("across"):
        half = jax.ShapeDtypeStruct((ROWS, HD), jnp.bfloat16)
        full = jax.ShapeDtypeStruct((ROWS, HD), jnp.float32)
        sent = [lax.ppermute(kv, "ctx", ctx_perm(dy=k)) for k in (1, -1, 2)]
        asked = lax.ppermute(query, "ctx", [(4 + y, y) for y in range(4)])
        args = (kv, *sent)
        helped, helped_stat = call(
            helped_kernel, (half, STATS), where, asked, *args, flops=2**30, moved=2**22, scratch=STATE
        )
        back = [(y, 4 + y) for y in range(4)]
        two, two_stat = (lax.ppermute(v, "ctx", back) for v in (helped, helped_stat))
        one, one_stat = call(
            across_kernel, (full, STATS), where, query, *args, flops=2**30, moved=2**22, scratch=STATE
        )
        return call(merge_kernel, half, where, one, one_stat, two, two_stat, moved=2**20)


def mix_kernel(where, *refs):
    blocks, (weights, out_ref, send_ref) = refs[:9], refs[9:]
    z, c = where[1], where[2]
    rows = [ref[...] for ref in blocks[:7]]
    rows.append(jnp.concatenate([blocks[7][...], blocks[8][...]], axis=0))
    acc = jnp.zeros((ROWS, 512), jnp.float32)
    for k in range(0, 8, 2):
        features = [
            weights[pl.ds(pl.multiple_of(jnp.bitwise_and(z + step, Z - 1) * HD, HD), HD), :]
            for step in STEPS[k : k + 2]
        ]
        acc += jnp.dot(
            jnp.concatenate(rows[k : k + 2], axis=1),
            jnp.concatenate(features, axis=0),
            preferred_element_type=jnp.float32,
        )
    first = c == 0
    for x in range(2):
        at = x * HD
        low, high = acc[:, 2 * at : 2 * at + HD], acc[:, 2 * at + HD : 2 * at + 2 * HD]
        out_ref[:, at : at + HD] = jnp.where(first, low, high)
        send_ref[:, at : at + HD] = jnp.where(first, high, low)


def split_kernel(where, own, came, out_ref, send_ref):
    low = own[:, :HD] + came[:, :HD]
    high = own[:, HD:] + came[:, HD:]
    first = where[0] == 0
    out_ref[...] = jnp.where(first, low, high)
    send_ref[...] = jnp.where(first, high, low).astype(send_ref.dtype)


def out_project(where, attn, weights, resid):
    with jax.named_scope("gather_attn"):
        blocks = along_z_all(attn)
    with jax.named_scope("mix"):
        pair = jax.ShapeDtypeStruct((ROWS, 2 * HD), jnp.float32)
        own, send = call(
            mix_kernel,
            (pair, pair),
            where,
            *blocks,
            weights,
            flops=2 * ROWS * 1024 * 512,
            moved=4 * 2**20,
        )
        came = to_other_core(send)
        own, send = call(
            split_kernel,
            (
                jax.ShapeDtypeStruct((ROWS, HD), jnp.float32),
                jax.ShapeDtypeStruct((ROWS, HD), jnp.bfloat16),
            ),
            where,
            own,
            came,
            moved=2**20,
        )
        summed = own + over_x(send).astype(jnp.float32)
        return (resid.astype(jnp.float32) + summed).astype(jnp.bfloat16)


def column_parts(out_one, out_two, index):
    with jax.named_scope("columns"):
        parts = [
            lax.dynamic_slice_in_dim(out, index * 16, 16, axis=0).reshape(16, 2, Z, 256)
            for out in (out_one, out_two)
        ]
        part = jnp.transpose(jnp.stack(parts), (3, 0, 1, 2, 4)).reshape(Z, 32, 512)
        groups = [
            [xh * 16 + z * 2 + c for z in range(Z)] for xh in range(2) for c in range(2)
        ]
        part = lax.all_to_all(part, "head", 0, 0, axis_index_groups=groups, tiled=True)
        return part[:, :16], part[:, 16:]


def column_rows(part):
    with jax.named_scope("columns"):
        return lax.all_gather(part, "ctx", axis=1, tiled=True).reshape(1024, 512)


def other_weights(planes, c):
    with jax.named_scope("swap"):
        split = planes.reshape(3, 16, 2, HD, HD)
        send = lax.dynamic_index_in_dim(split, 1 - c, axis=2, keepdims=False)
        return to_other_core(send.reshape(3, 2048, HD))


def local(tokens, lengths, gain_one, qkv_one, out_one, gain_two, qkv_two, out_two):
    index = lax.axis_index("ctx").astype(jnp.int32)
    head = lax.axis_index("head").astype(jnp.int32)
    c = head % 2
    where = jnp.stack([head // 16, (head // 2) % Z, c, index // 4, index % 4, index])

    planes_one = jnp.transpose(qkv_one, (1, 0, 2))
    planes_two = jnp.transpose(qkv_two, (1, 0, 2))
    order = jnp.arange(lengths.shape[0])
    ends = jnp.sum(jnp.where(order[None, :] <= order[:, None], lengths[None, :], 0), axis=1)
    own_pos = index * ROWS + jnp.arange(ROWS, dtype=jnp.int32)
    starts = jnp.max(
        jnp.where(ends[None, :] <= own_pos[:, None], ends[None, :], 0), axis=1, keepdims=True
    )

    part_one, part_two = column_parts(out_one, out_two, index)
    with jax.named_scope("gather_tokens"):
        pair = jnp.concatenate([tokens, over_x(tokens)], axis=0)
        pair = after(pair, part_one, part_two)
        columns_one = column_rows(part_one)
        columns_two = column_rows(part_two)
        others_one = other_weights(after(planes_one, pair), c)
        blocks = along_z_all(pair)
    query, kv = project(where, blocks, gain_one, planes_one, others_one)
    half = jax.ShapeDtypeStruct((ROWS, HD), jnp.bfloat16)
    with jax.named_scope("within"):
        prev = lax.ppermute(kv, "ctx", [(i, i + 1) for i in range(7)])
        attn = call(within_kernel, half, where, starts, query, kv, prev, flops=2**28, moved=2**20)
    others_two = other_weights(after(planes_two, attn), c)
    stream = out_project(where, attn, columns_one, tokens)

    with jax.named_scope("gather_stream"):
        stream = after(stream, columns_two, others_two)
        blocks = along_z_all(jnp.concatenate([stream, over_x(stream)], axis=0))
    query, kv = project(where, blocks, gain_two, planes_two, others_two)
    attn = across(where, query, kv)
    return out_project(where, attn, columns_two, stream)


def solution(mesh):
    placed = (
        P("ctx", "head"),
        P(),
        P(),
        P(None, None, "head"),
        P("head", None),
        P(),
        P(None, None, "head"),
        P("head", None),
    )
    return jax.shard_map(
        local, mesh=mesh, in_specs=placed, out_specs=P("ctx", "head"), check_vma=False
    )
```

```python
import jax
import jax.numpy as jnp
import numpy as np
from jax import lax
from jax.experimental import pallas as pl
from jax.experimental.pallas import tpu as pltpu
from jax.sharding import PartitionSpec as P

HD = 128
EPS = 1e-05
D = 4096
ROWS = 512
Z = 8
SCALE = HD ** (-0.5) * 1.4426950408889634
STEPS = (0, -1, 1, -2, 2, -3, 3, 4)
ANYWHERE = pl.BlockSpec(memory_space=pltpu.VMEM)
SCALARS = pl.BlockSpec(memory_space=pltpu.SMEM)


def call(kernel, out, *args, flops=0, moved=0, scratch=(), scalars=1, limit=12):
    return pl.pallas_call(
        kernel,
        out_shape=out,
        in_specs=[SCALARS] * scalars + [ANYWHERE] * (len(args) - scalars),
        out_specs=jax.tree.map(lambda _: ANYWHERE, out),
        scratch_shapes=list(scratch),
        compiler_params=pltpu.CompilerParams(vmem_limit_bytes=limit * 2**20),
        cost_estimate=pl.CostEstimate(flops=flops, bytes_accessed=moved, transcendentals=0),
    )(*args)


def head_perm(dxh=0, dz=0, dc=0):
    pairs = []
    for xh in range(2):
        for z in range(Z):
            for c in range(2):
                to = ((xh + dxh) % 2) * 16 + ((z + dz) % Z) * 2 + (c + dc) % 2
                pairs.append((xh * 16 + z * 2 + c, to))
    return pairs


def ctx_perm(dxl=0, dy=0):
    return [
        (xl * 4 + y, ((xl + dxl) % 2) * 4 + (y + dy) % 4) for xl in range(2) for y in range(4)
    ]


def along_z(value, steps):
    return lax.ppermute(value, "head", head_perm(dz=steps))


def to_other_core(value):
    return lax.ppermute(value, "head", head_perm(dc=1))


def along_z_all(block):
    half = block.shape[0] // 2
    f1, b1, f2, b2 = (along_z(block, k) for k in (1, -1, 2, -2))
    f3, b3 = along_z(f2, 1), along_z(b2, -1)
    g1, g2 = along_z(f2[:half], 2), along_z(b2[half:], -2)
    return (block, f1, b1, f2, b2, f3, b3, g1, g2)


def over_x(value):
    return lax.ppermute(value, "head", head_perm(dxh=1))


def after(value, *others):
    return lax.optimization_barrier((value, others))[0]


def product(where, parts, gain, mine, others):
    xh, z, c = where[0], where[1], where[2]
    acc = jnp.zeros((ROWS, 768), jnp.float32)
    squares = jnp.zeros((ROWS, HD), jnp.float32)
    for step, one, two in parts:
        at = jnp.bitwise_and(z + step, Z - 1)
        scaled, weights = [], []
        for rows, x in ((one, xh), (two, 1 - xh)):
            wide = rows.astype(jnp.float32)
            squares += wide * wide
            chip = x * Z + at
            head = chip * 2 + c
            scaled.append((wide * gain[pl.ds(head, 1), :]).astype(jnp.bfloat16))
            first = pl.multiple_of(head * HD, HD)
            half = pl.multiple_of(chip * HD, HD)
            weights.append(
                jnp.concatenate(
                    [mine[t, pl.ds(first, HD), :] for t in range(3)]
                    + [others[t, pl.ds(half, HD), :] for t in range(3)],
                    axis=1,
                )
            )
        acc += jnp.dot(
            jnp.concatenate(scaled, axis=1),
            jnp.concatenate(weights, axis=0),
            preferred_element_type=jnp.float32,
        )
    return acc, squares


def project_early(where, *refs):
    blocks, (gain, mine, others, acc_ref, squares_ref) = refs[:5], refs[5:]
    parts = [(k, ref[:ROWS, :], ref[ROWS:, :]) for k, ref in zip(STEPS, blocks)]
    acc_ref[...], squares_ref[...] = product(where, parts, gain, mine, others)


def project_late(where, *refs):
    blocks, (acc_early, squares_early, gain, mine, others, out_ref, send_ref) = refs[:4], refs[4:]
    parts = [(k, ref[:ROWS, :], ref[ROWS:, :]) for k, ref in zip(STEPS[5:], blocks[:2])]
    parts.append((STEPS[7], blocks[2][...], blocks[3][...]))
    acc, squares = product(where, parts, gain, mine, others)
    acc += acc_early[...]
    squares += squares_early[...]
    total = jnp.broadcast_to(jnp.sum(squares, axis=1, keepdims=True), (ROWS, HD))
    out_ref[:, :384] = acc[:, :384]
    out_ref[:, 384:] = total
    send_ref[:, :384] = acc[:, 384:]
    send_ref[:, 384:] = total


def finish_kernel(where, own, came, q_ref, kv_ref):
    total = own[:, 384:] + came[:, 384:]
    factor = lax.rsqrt(total * (1.0 / D) + EPS)
    q_ref[...] = ((own[:, :128] + came[:, :128]) * factor).astype(jnp.bfloat16)
    kv_ref[:, :128] = ((own[:, 128:256] + came[:, 128:256]) * factor).astype(jnp.bfloat16)
    kv_ref[:, 128:] = ((own[:, 256:384] + came[:, 256:384]) * factor).astype(jnp.bfloat16)


def project(where, blocks, gain, mine, others):
    with jax.named_scope("project"):
        gain = gain.reshape(32, HD)
        early = call(
            project_early,
            (
                jax.ShapeDtypeStruct((ROWS, 768), jnp.float32),
                jax.ShapeDtypeStruct((ROWS, HD), jnp.float32),
            ),
            where,
            *blocks[:5],
            gain,
            mine,
            others,
            flops=2 * ROWS * 1280 * 768,
            moved=6 * 2**20,
        )
        wide = jax.ShapeDtypeStruct((ROWS, 512), jnp.float32)
        own, send = call(
            project_late,
            (wide, wide),
            where,
            *blocks[5:],
            *early,
            gain,
            mine,
            others,
            flops=2 * ROWS * 768 * 768,
            moved=6 * 2**20,
        )
        came = to_other_core(send)
        return call(
            finish_kernel,
            (
                jax.ShapeDtypeStruct((ROWS, HD), jnp.bfloat16),
                jax.ShapeDtypeStruct((ROWS, 2 * HD), jnp.bfloat16),
            ),
            where,
            own,
            came,
            moved=3 * 2**20,
        )


def scores_of(query, keys):
    return (
        lax.dot_general(query, keys, (((1,), (1,)), ((), ())), preferred_element_type=jnp.float32)
        * SCALE
    )


def within_kernel(where, lengths, q_ref, kv_ref, prev_ref, out_ref):
    query = q_ref[...]
    first = where[5] * ROWS
    place = lax.broadcasted_iota(jnp.int32, (8, ROWS), 1) + first
    start = jnp.zeros((8, ROWS), jnp.int32)
    end = jnp.int32(0)
    for s in range(lengths.shape[0]):
        end = end + lengths[s]
        start = jnp.where(end <= place, end, start)
    start = jnp.broadcast_to(start[:1, :].astype(jnp.float32), (HD, ROWS))
    start = jnp.transpose(start)[:, :1].astype(jnp.int32)
    row = lax.broadcasted_iota(jnp.int32, (ROWS, ROWS), 0) + first
    col = lax.broadcasted_iota(jnp.int32, (ROWS, ROWS), 1) + first
    ok_own = (col <= row) & (col >= start)
    ok_prev = (col - ROWS) >= start
    s_own = jnp.where(ok_own, scores_of(query, kv_ref[:, :HD]), -1e30)
    s_prev = jnp.where(ok_prev, scores_of(query, prev_ref[:, :HD]), -1e30)
    top = jnp.maximum(
        jnp.max(s_own, axis=1, keepdims=True), jnp.max(s_prev, axis=1, keepdims=True)
    )
    e_own = jnp.exp2(s_own - top)
    e_prev = jnp.exp2(s_prev - top)
    total = jnp.sum(e_own, axis=1, keepdims=True) + jnp.sum(e_prev, axis=1, keepdims=True)
    mixed = jnp.dot(
        e_own.astype(jnp.bfloat16), kv_ref[:, HD:], preferred_element_type=jnp.float32
    ) + jnp.dot(e_prev.astype(jnp.bfloat16), prev_ref[:, HD:], preferred_element_type=jnp.float32)
    out_ref[...] = (mixed / total).astype(jnp.bfloat16)


def start_state(query, keys, values, state):
    s = scores_of(query, keys)
    row = lax.broadcasted_iota(jnp.int32, (ROWS, ROWS), 0)
    col = lax.broadcasted_iota(jnp.int32, (ROWS, ROWS), 1)
    s = jnp.where(col <= row, s, -1e30)
    top = jnp.max(s, axis=1, keepdims=True)
    expo = jnp.exp2(s - top)
    state[0][...] = top
    state[1][...] = jnp.sum(expo, axis=1, keepdims=True)
    state[2][...] = jnp.dot(expo.astype(jnp.bfloat16), values, preferred_element_type=jnp.float32)


def add_keys(query, keys, values, state):
    s = scores_of(query, keys)
    old = state[0][...]
    top = jnp.maximum(old, jnp.max(s, axis=1, keepdims=True))
    expo = jnp.exp2(s - top)
    shrink = jnp.exp2(old - top)
    state[0][...] = top
    state[1][...] = state[1][...] * shrink + jnp.sum(expo, axis=1, keepdims=True)
    state[2][...] = state[2][...] * shrink + jnp.dot(
        expo.astype(jnp.bfloat16), values, preferred_element_type=jnp.float32
    )


STATE = (
    pltpu.VMEM((ROWS, 1), jnp.float32),
    pltpu.VMEM((ROWS, 1), jnp.float32),
    pltpu.VMEM((ROWS, HD), jnp.float32),
)
STATS = jax.ShapeDtypeStruct((8, ROWS), jnp.float32)


def give(state, out_ref, stat_ref):
    total = state[1][...]
    out_ref[...] = (state[2][...] / total).astype(out_ref.dtype)
    lane = lax.broadcasted_iota(jnp.int32, (ROWS, HD), 1)
    both = jnp.where(lane == 0, state[0][...], total)
    stat_ref[...] = jnp.transpose(both)[:8, :]


def helped_kernel(where, q_ref, kv0, kv1, kv2, kv3, out_ref, stat_ref, *state):
    @pl.when(where[3] == 0)
    def _():
        query = q_ref[...]
        state[0][...] = jnp.full((ROWS, 1), -1e30, jnp.float32)
        state[1][...] = jnp.zeros((ROWS, 1), jnp.float32)
        state[2][...] = jnp.zeros((ROWS, HD), jnp.float32)
        for ref in (kv0, kv1, kv2, kv3):
            add_keys(query, ref[:, :HD], ref[:, HD:], state)
        give(state, out_ref, stat_ref)

    @pl.when(where[3] != 0)
    def _():
        out_ref[...] = jnp.zeros((ROWS, HD), out_ref.dtype)
        stat_ref[...] = jnp.zeros((8, ROWS), jnp.float32)


def across_kernel(where, q_ref, kv0, kv1, kv2, kv3, out_ref, stat_ref, *state):
    y = where[4]
    query = q_ref[...]
    start_state(query, kv0[:, :HD], kv0[:, HD:], state)
    for ref, dy in ((kv1, -1), (kv2, 1), (kv3, 2)):

        @pl.when(jnp.bitwise_and(y + dy, 3) < y)
        def _(ref=ref):
            add_keys(query, ref[:, :HD], ref[:, HD:], state)

    give(state, out_ref, stat_ref)


def merge_kernel(where, one, stat_one, two, stat_two, out_ref):
    a, b = stat_one[...], stat_two[...]
    second = where[3] != 0
    top_a, total_a = a[0:1, :], a[1:2, :]
    top_b = jnp.where(second, b[0:1, :], -1e30)
    total_b = jnp.where(second, b[1:2, :], 0.0)
    top = jnp.maximum(top_a, top_b)
    share_a = total_a * jnp.exp2(top_a - top)
    share_b = total_b * jnp.exp2(top_b - top)
    part = share_b / (share_a + share_b)
    part = jnp.transpose(jnp.broadcast_to(part, (HD, ROWS)))
    first = one[...]
    out_ref[...] = (first + (two[...].astype(jnp.float32) - first) * part).astype(jnp.bfloat16)


def across(where, query, kv):
    with jax.named_scope("across"):
        half = jax.ShapeDtypeStruct((ROWS, HD), jnp.bfloat16)
        full = jax.ShapeDtypeStruct((ROWS, HD), jnp.float32)
        sent = [lax.ppermute(kv, "ctx", ctx_perm(dy=k)) for k in (1, -1, 2)]
        asked = lax.ppermute(query, "ctx", [(4 + y, y) for y in range(4)])
        args = (kv, *sent)
        helped, helped_stat = call(
            helped_kernel, (half, STATS), where, asked, *args, flops=2**30, moved=2**22, scratch=STATE
        )
        back = [(y, 4 + y) for y in range(4)]
        two, two_stat = (lax.ppermute(v, "ctx", back) for v in (helped, helped_stat))
        one, one_stat = call(
            across_kernel, (full, STATS), where, query, *args, flops=2**30, moved=2**22, scratch=STATE
        )
        return call(merge_kernel, half, where, one, one_stat, two, two_stat, moved=2**20)


def mixed(where, rows, steps, weights):
    z = where[1]
    acc = jnp.zeros((ROWS, 512), jnp.float32)
    for k in range(0, len(steps), 2):
        features = [
            weights[pl.ds(pl.multiple_of(jnp.bitwise_and(z + step, Z - 1) * HD, HD), HD), :]
            for step in steps[k : k + 2]
        ]
        acc += jnp.dot(
            jnp.concatenate(rows[k : k + 2], axis=1),
            jnp.concatenate(features, axis=0),
            preferred_element_type=jnp.float32,
        )
    return acc


def mix_early(where, r0, r1, r2, r3, weights, acc_ref):
    rows = [ref[...] for ref in (r0, r1, r2, r3)]
    acc_ref[...] = mixed(where, rows, STEPS[:4], weights)


def mix_late(where, r4, r5, r6, low, high, early, weights, out_ref, send_ref):
    rows = [ref[...] for ref in (r4, r5, r6)]
    rows.append(jnp.concatenate([low[...], high[...]], axis=0))
    acc = early[...] + mixed(where, rows, STEPS[4:], weights)
    first = where[2] == 0
    for x in range(2):
        at = x * HD
        low, high = acc[:, 2 * at : 2 * at + HD], acc[:, 2 * at + HD : 2 * at + 2 * HD]
        out_ref[:, at : at + HD] = jnp.where(first, low, high)
        send_ref[:, at : at + HD] = jnp.where(first, high, low)


def split_kernel(where, own, came, out_ref, send_ref):
    low = own[:, :HD] + came[:, :HD]
    high = own[:, HD:] + came[:, HD:]
    first = where[0] == 0
    out_ref[...] = jnp.where(first, low, high)
    send_ref[...] = jnp.where(first, high, low).astype(send_ref.dtype)


def half_sum_kernel(where, own, came, out_ref):
    out_ref[...] = (own[...] + came[...]).astype(out_ref.dtype)


def pair_kernel(where, one, two, resid, out_ref):
    low = one[:, :HD].astype(jnp.float32) + two[:, :HD].astype(jnp.float32)
    high = one[:, HD:].astype(jnp.float32) + two[:, HD:].astype(jnp.float32)
    first = where[0] == 0
    own, other = jnp.where(first, low, high), jnp.where(first, high, low)
    out_ref[:ROWS, :] = (resid[:ROWS, :].astype(jnp.float32) + own).astype(jnp.bfloat16)
    out_ref[ROWS:, :] = (resid[ROWS:, :].astype(jnp.float32) + other).astype(jnp.bfloat16)


def mix(where, attn, weights):
    with jax.named_scope("gather_attn"):
        blocks = along_z_all(attn)
    with jax.named_scope("mix"):
        early = call(
            mix_early,
            jax.ShapeDtypeStruct((ROWS, 512), jnp.float32),
            where,
            *blocks[:4],
            weights,
            flops=2 * ROWS * 512 * 512,
            moved=2**21,
        )
        pair = jax.ShapeDtypeStruct((ROWS, 2 * HD), jnp.float32)
        own, send = call(
            mix_late,
            (pair, pair),
            where,
            *blocks[4:],
            early,
            weights,
            flops=2 * ROWS * 512 * 512,
            moved=2**21,
        )
        return own, to_other_core(send)


def mix_to_pair(where, attn, weights, resid):
    sums = mix(where, attn, weights)
    with jax.named_scope("mix"):
        halves = jax.ShapeDtypeStruct((ROWS, 2 * HD), jnp.bfloat16)
        one = call(half_sum_kernel, halves, where, *sums, moved=2**20)
        pair = jax.ShapeDtypeStruct((2 * ROWS, HD), jnp.bfloat16)
        return call(pair_kernel, pair, where, one, over_x(one), resid, moved=2**20)


def mix_to_own(where, attn, weights, resid):
    sums = mix(where, attn, weights)
    with jax.named_scope("mix"):
        own, send = call(
            split_kernel,
            (
                jax.ShapeDtypeStruct((ROWS, HD), jnp.float32),
                jax.ShapeDtypeStruct((ROWS, HD), jnp.bfloat16),
            ),
            where,
            *sums,
            moved=2**20,
        )
        summed = own + over_x(send).astype(jnp.float32)
        return (resid.astype(jnp.float32) + summed).astype(jnp.bfloat16)


def part_kernel(where, one, two, out_ref):
    for m, ref in enumerate((one, two)):
        for xh in range(2):
            for z in range(Z):
                at = (xh * Z + z) * 256
                out_ref[z, m * 16 : m * 16 + 16, xh * 256 : xh * 256 + 256] = ref[:, at : at + 256]


def column_part(where, out_one, out_two):
    with jax.named_scope("columns"):
        rows = pl.BlockSpec((16, D), lambda step, at: (at[5], 0))
        part = pl.pallas_call(
            part_kernel,
            out_shape=jax.ShapeDtypeStruct((Z, 32, 512), jnp.bfloat16),
            grid_spec=pltpu.PrefetchScalarGridSpec(
                num_scalar_prefetch=1,
                grid=(1,),
                in_specs=[rows, rows],
                out_specs=pl.BlockSpec((Z, 32, 512), lambda step, at: (0, 0, 0)),
            ),
            compiler_params=pltpu.CompilerParams(vmem_limit_bytes=4 * 2**20),
        )(where, out_one, out_two)
        groups = [[xh * 16 + z * 2 + c for z in range(Z)] for xh in range(2) for c in range(2)]
        return lax.all_to_all(part, "head", 0, 0, axis_index_groups=groups, tiled=True)


def column_rows(part):
    with jax.named_scope("columns"):
        return lax.all_gather(part, "ctx", axis=1, tiled=True).reshape(1024, 512)


def other_weights(planes, c):
    with jax.named_scope("swap"):
        split = planes.reshape(3, 16, 2, HD, HD)
        send = lax.dynamic_index_in_dim(split, 1 - c, axis=2, keepdims=False)
        return to_other_core(send.reshape(3, 2048, HD))


def local(tokens, lengths, gain_one, qkv_one, out_one, gain_two, qkv_two, out_two):
    index = lax.axis_index("ctx").astype(jnp.int32)
    head = lax.axis_index("head").astype(jnp.int32)
    c = head % 2
    at = jnp.where(jnp.arange(6) < 3, head, index)
    where = jnp.right_shift(at, np.array([4, 1, 0, 2, 0, 0])) & np.array([1, 7, 1, 1, 3, 7])

    planes_one = jnp.transpose(qkv_one, (1, 0, 2))
    planes_two = jnp.transpose(qkv_two, (1, 0, 2))
    with jax.named_scope("gather_tokens"):
        part = column_part(where, out_one, out_two)
        tokens_pair = jnp.concatenate([tokens, over_x(tokens)], axis=0)
        others_one = other_weights(after(planes_one, tokens_pair), c)
        tokens_pair = after(tokens_pair, part)
        columns_one = column_rows(part[:, :16])
        blocks = along_z_all(tokens_pair)
    query, kv = project(where, blocks, gain_one, planes_one, others_one)
    half = jax.ShapeDtypeStruct((ROWS, HD), jnp.bfloat16)
    with jax.named_scope("within"):
        prev = lax.ppermute(kv, "ctx", [(i, i + 1) for i in range(7)])
        others_two = other_weights(after(planes_two, kv), c)
        prev = after(prev, columns_one)
        attn = call(
            within_kernel, half, where, lengths, query, kv, prev, flops=2**28, moved=2**20, scalars=2
        )
    columns_two = column_rows(after(part[:, 16:], attn))
    pair = mix_to_pair(where, attn, columns_one, tokens_pair)

    with jax.named_scope("gather_stream"):
        pair = after(pair, columns_two, others_two)
        blocks = along_z_all(pair)
    query, kv = project(where, blocks, gain_two, planes_two, others_two)
    attn = across(where, query, kv)
    return mix_to_own(where, attn, columns_two, pair[:ROWS])


def solution(mesh):
    placed = (
        P("ctx", "head"),
        P(),
        P(),
        P(None, None, "head"),
        P("head", None),
        P(),
        P(None, None, "head"),
        P("head", None),
    )
    return jax.shard_map(
        local, mesh=mesh, in_specs=placed, out_specs=P("ctx", "head"), check_vma=False
    )
```

```python
import jax
import jax.numpy as jnp
import numpy as np
from jax import lax
from jax.experimental import pallas as pl
from jax.experimental.pallas import tpu as pltpu
from jax.sharding import PartitionSpec as P

HD = 128
EPS = 1e-05
D = 4096
ROWS = 512
Z = 8
SCALE = HD ** (-0.5) * 1.4426950408889634
STEPS = (0, -1, 1, -2, 2, -3, 3, 4)
ANYWHERE = pl.BlockSpec(memory_space=pltpu.VMEM)
SCALARS = pl.BlockSpec(memory_space=pltpu.SMEM)


def call(kernel, out, *args, flops=0, moved=0, scratch=(), scalars=1, limit=12):
    return pl.pallas_call(
        kernel,
        out_shape=out,
        in_specs=[SCALARS] * scalars + [ANYWHERE] * (len(args) - scalars),
        out_specs=jax.tree.map(lambda _: ANYWHERE, out),
        scratch_shapes=list(scratch),
        compiler_params=pltpu.CompilerParams(vmem_limit_bytes=limit * 2**20),
        cost_estimate=pl.CostEstimate(flops=flops, bytes_accessed=moved, transcendentals=0),
    )(*args)


def head_perm(dxh=0, dz=0, dc=0):
    pairs = []
    for xh in range(2):
        for z in range(Z):
            for c in range(2):
                to = ((xh + dxh) % 2) * 16 + ((z + dz) % Z) * 2 + (c + dc) % 2
                pairs.append((xh * 16 + z * 2 + c, to))
    return pairs


def ctx_perm(dxl=0, dy=0):
    return [
        (xl * 4 + y, ((xl + dxl) % 2) * 4 + (y + dy) % 4) for xl in range(2) for y in range(4)
    ]


def along_z(value, steps):
    return lax.ppermute(value, "head", head_perm(dz=steps))


def to_other_core(value):
    return lax.ppermute(value, "head", head_perm(dc=1))


def along_z_all(block):
    half = block.shape[0] // 2
    f1, b1, f2, b2 = (along_z(block, k) for k in (1, -1, 2, -2))
    f3, b3 = along_z(f2, 1), along_z(b2, -1)
    g1, g2 = along_z(f2[:half], 2), along_z(b2[half:], -2)
    return (block, f1, b1, f2, b2, f3, b3, g1, g2)


def over_x(value):
    return lax.ppermute(value, "head", head_perm(dxh=1))


def after(value, *others):
    return lax.optimization_barrier((value, others))[0]


def product(where, parts, gain, mine, others):
    xh, z, c = where[0], where[1], where[2]
    acc = jnp.zeros((ROWS, 768), jnp.float32)
    squares = jnp.zeros((ROWS, HD), jnp.float32)
    for step, one, two in parts:
        at = jnp.bitwise_and(z + step, Z - 1)
        scaled, weights = [], []
        for rows, x in ((one, xh), (two, 1 - xh)):
            wide = rows.astype(jnp.float32)
            squares += wide * wide
            head = (x * Z + at) * 2 + c
            scaled.append((wide * gain[pl.ds(head, 1), :]).astype(jnp.bfloat16))
            first = pl.multiple_of(head * HD, HD)
            weights.append(
                jnp.concatenate(
                    [mine[t, pl.ds(first, HD), :] for t in range(3)]
                    + [others[t, pl.ds(first, HD), :] for t in range(3)],
                    axis=1,
                )
            )
        acc += jnp.dot(
            jnp.concatenate(scaled, axis=1),
            jnp.concatenate(weights, axis=0),
            preferred_element_type=jnp.float32,
        )
    return acc, squares


def project_early(where, *refs):
    blocks, (gain, mine, others, acc_ref, squares_ref) = refs[:5], refs[5:]
    parts = [(k, ref[:ROWS, :], ref[ROWS:, :]) for k, ref in zip(STEPS, blocks)]
    acc_ref[...], squares_ref[...] = product(where, parts, gain, mine, others)


def project_late(where, *refs):
    blocks, (acc_early, squares_early, gain, mine, others, out_ref, send_ref) = refs[:4], refs[4:]
    parts = [(k, ref[:ROWS, :], ref[ROWS:, :]) for k, ref in zip(STEPS[5:], blocks[:2])]
    parts.append((STEPS[7], blocks[2][...], blocks[3][...]))
    acc, squares = product(where, parts, gain, mine, others)
    acc += acc_early[...]
    squares += squares_early[...]
    total = jnp.broadcast_to(jnp.sum(squares, axis=1, keepdims=True), (ROWS, HD))
    out_ref[:, :384] = acc[:, :384]
    out_ref[:, 384:] = total
    send_ref[:, :384] = acc[:, 384:]
    send_ref[:, 384:] = total


def finish_kernel(where, own, came, q_ref, kv_ref):
    total = own[:, 384:] + came[:, 384:]
    factor = lax.rsqrt(total * (1.0 / D) + EPS)
    q_ref[...] = ((own[:, :128] + came[:, :128]) * factor).astype(jnp.bfloat16)
    kv_ref[:, :128] = ((own[:, 128:256] + came[:, 128:256]) * factor).astype(jnp.bfloat16)
    kv_ref[:, 128:] = ((own[:, 256:384] + came[:, 256:384]) * factor).astype(jnp.bfloat16)


def project(where, blocks, gain, mine, others):
    with jax.named_scope("project"):
        gain = gain.reshape(32, HD)
        early = call(
            project_early,
            (
                jax.ShapeDtypeStruct((ROWS, 768), jnp.float32),
                jax.ShapeDtypeStruct((ROWS, HD), jnp.float32),
            ),
            where,
            *blocks[:5],
            gain,
            mine,
            others,
            flops=2 * ROWS * 1280 * 768,
            moved=6 * 2**20,
        )
        wide = jax.ShapeDtypeStruct((ROWS, 512), jnp.float32)
        own, send = call(
            project_late,
            (wide, wide),
            where,
            *blocks[5:],
            *early,
            gain,
            mine,
            others,
            flops=2 * ROWS * 768 * 768,
            moved=6 * 2**20,
        )
        came = to_other_core(send)
        return call(
            finish_kernel,
            (
                jax.ShapeDtypeStruct((ROWS, HD), jnp.bfloat16),
                jax.ShapeDtypeStruct((ROWS, 2 * HD), jnp.bfloat16),
            ),
            where,
            own,
            came,
            moved=3 * 2**20,
        )


def scores_of(query, keys):
    return (
        lax.dot_general(query, keys, (((1,), (1,)), ((), ())), preferred_element_type=jnp.float32)
        * SCALE
    )


def within_kernel(where, lengths, q_ref, kv_ref, prev_ref, out_ref):
    query = q_ref[...]
    first = where[5] * ROWS
    place = lax.broadcasted_iota(jnp.int32, (8, ROWS), 1) + first
    start = jnp.zeros((8, ROWS), jnp.int32)
    end = jnp.int32(0)
    for s in range(lengths.shape[0]):
        end = end + lengths[s]
        start = jnp.where(end <= place, end, start)
    start = jnp.broadcast_to(start[:1, :].astype(jnp.float32), (HD, ROWS))
    start = jnp.transpose(start)[:, :1].astype(jnp.int32)
    row = lax.broadcasted_iota(jnp.int32, (ROWS, ROWS), 0) + first
    col = lax.broadcasted_iota(jnp.int32, (ROWS, ROWS), 1) + first
    ok_own = (col <= row) & (col >= start)
    ok_prev = (col - ROWS) >= start
    s_own = jnp.where(ok_own, scores_of(query, kv_ref[:, :HD]), -1e30)
    s_prev = jnp.where(ok_prev, scores_of(query, prev_ref[:, :HD]), -1e30)
    top = jnp.maximum(
        jnp.max(s_own, axis=1, keepdims=True), jnp.max(s_prev, axis=1, keepdims=True)
    )
    e_own = jnp.exp2(s_own - top)
    e_prev = jnp.exp2(s_prev - top)
    total = jnp.sum(e_own, axis=1, keepdims=True) + jnp.sum(e_prev, axis=1, keepdims=True)
    mixed = jnp.dot(
        e_own.astype(jnp.bfloat16), kv_ref[:, HD:], preferred_element_type=jnp.float32
    ) + jnp.dot(e_prev.astype(jnp.bfloat16), prev_ref[:, HD:], preferred_element_type=jnp.float32)
    out_ref[...] = (mixed / total).astype(jnp.bfloat16)


def start_state(query, keys, values, state):
    s = scores_of(query, keys)
    row = lax.broadcasted_iota(jnp.int32, (ROWS, ROWS), 0)
    col = lax.broadcasted_iota(jnp.int32, (ROWS, ROWS), 1)
    s = jnp.where(col <= row, s, -1e30)
    top = jnp.max(s, axis=1, keepdims=True)
    expo = jnp.exp2(s - top)
    state[0][...] = top
    state[1][...] = jnp.sum(expo, axis=1, keepdims=True)
    state[2][...] = jnp.dot(expo.astype(jnp.bfloat16), values, preferred_element_type=jnp.float32)


def add_keys(query, keys, values, state):
    s = scores_of(query, keys)
    old = state[0][...]
    top = jnp.maximum(old, jnp.max(s, axis=1, keepdims=True))
    expo = jnp.exp2(s - top)
    shrink = jnp.exp2(old - top)
    state[0][...] = top
    state[1][...] = state[1][...] * shrink + jnp.sum(expo, axis=1, keepdims=True)
    state[2][...] = state[2][...] * shrink + jnp.dot(
        expo.astype(jnp.bfloat16), values, preferred_element_type=jnp.float32
    )


STATE = (
    pltpu.VMEM((ROWS, 1), jnp.float32),
    pltpu.VMEM((ROWS, 1), jnp.float32),
    pltpu.VMEM((ROWS, HD), jnp.float32),
)
STATS = jax.ShapeDtypeStruct((8, ROWS), jnp.float32)


def give(state, out_ref, stat_ref):
    total = state[1][...]
    out_ref[...] = (state[2][...] / total).astype(out_ref.dtype)
    lane = lax.broadcasted_iota(jnp.int32, (ROWS, HD), 1)
    both = jnp.where(lane == 0, state[0][...], total)
    stat_ref[...] = jnp.transpose(both)[:8, :]


def helped_kernel(where, q_ref, kv0, kv1, kv2, kv3, out_ref, stat_ref, *state):
    @pl.when(where[3] == 0)
    def _():
        query = q_ref[...]
        state[0][...] = jnp.full((ROWS, 1), -1e30, jnp.float32)
        state[1][...] = jnp.zeros((ROWS, 1), jnp.float32)
        state[2][...] = jnp.zeros((ROWS, HD), jnp.float32)
        for ref in (kv0, kv1, kv2, kv3):
            add_keys(query, ref[:, :HD], ref[:, HD:], state)
        give(state, out_ref, stat_ref)

    @pl.when(where[3] != 0)
    def _():
        out_ref[...] = jnp.zeros((ROWS, HD), out_ref.dtype)
        stat_ref[...] = jnp.zeros((8, ROWS), jnp.float32)


def across_kernel(where, q_ref, kv0, kv1, kv2, kv3, out_ref, stat_ref, *state):
    y = where[4]
    query = q_ref[...]
    start_state(query, kv0[:, :HD], kv0[:, HD:], state)
    for ref, dy in ((kv1, -1), (kv2, 1), (kv3, 2)):

        @pl.when(jnp.bitwise_and(y + dy, 3) < y)
        def _(ref=ref):
            add_keys(query, ref[:, :HD], ref[:, HD:], state)

    give(state, out_ref, stat_ref)


def merge_kernel(where, one, stat_one, two, stat_two, out_ref):
    a, b = stat_one[...], stat_two[...]
    second = where[3] != 0
    top_a, total_a = a[0:1, :], a[1:2, :]
    top_b = jnp.where(second, b[0:1, :], -1e30)
    total_b = jnp.where(second, b[1:2, :], 0.0)
    top = jnp.maximum(top_a, top_b)
    share_a = total_a * jnp.exp2(top_a - top)
    share_b = total_b * jnp.exp2(top_b - top)
    part = share_b / (share_a + share_b)
    part = jnp.transpose(jnp.broadcast_to(part, (HD, ROWS)))
    first = one[...]
    out_ref[...] = (first + (two[...].astype(jnp.float32) - first) * part).astype(jnp.bfloat16)


def across(where, query, kv):
    with jax.named_scope("across"):
        half = jax.ShapeDtypeStruct((ROWS, HD), jnp.bfloat16)
        full = jax.ShapeDtypeStruct((ROWS, HD), jnp.float32)
        sent = [lax.ppermute(kv, "ctx", ctx_perm(dy=k)) for k in (1, -1, 2)]
        asked = lax.ppermute(query, "ctx", [(4 + y, y) for y in range(4)])
        args = (kv, *sent)
        helped, helped_stat = call(
            helped_kernel, (half, STATS), where, asked, *args, flops=2**30, moved=2**22, scratch=STATE
        )
        back = [(y, 4 + y) for y in range(4)]
        two, two_stat = (lax.ppermute(v, "ctx", back) for v in (helped, helped_stat))
        one, one_stat = call(
            across_kernel, (full, STATS), where, query, *args, flops=2**30, moved=2**22, scratch=STATE
        )
        return call(merge_kernel, half, where, one, one_stat, two, two_stat, moved=2**20)


def mixed(where, rows, steps, weights):
    z = where[1]
    acc = jnp.zeros((ROWS, 512), jnp.float32)
    for k in range(0, len(steps), 2):
        features = [
            weights[pl.ds(pl.multiple_of(jnp.bitwise_and(z + step, Z - 1) * HD, HD), HD), :]
            for step in steps[k : k + 2]
        ]
        acc += jnp.dot(
            jnp.concatenate(rows[k : k + 2], axis=1),
            jnp.concatenate(features, axis=0),
            preferred_element_type=jnp.float32,
        )
    return acc


def mix_early(where, r0, r1, r2, r3, weights, acc_ref):
    rows = [ref[...] for ref in (r0, r1, r2, r3)]
    acc_ref[...] = mixed(where, rows, STEPS[:4], weights)


def mix_late(where, r4, r5, r6, low, high, early, weights, out_ref, send_ref):
    rows = [ref[...] for ref in (r4, r5, r6)]
    rows.append(jnp.concatenate([low[...], high[...]], axis=0))
    acc = early[...] + mixed(where, rows, STEPS[4:], weights)
    first = where[2] == 0
    for x in range(2):
        at = x * HD
        low, high = acc[:, 2 * at : 2 * at + HD], acc[:, 2 * at + HD : 2 * at + 2 * HD]
        out_ref[:, at : at + HD] = jnp.where(first, low, high)
        send_ref[:, at : at + HD] = jnp.where(first, high, low)


def split_kernel(where, own, came, out_ref, send_ref):
    low = own[:, :HD] + came[:, :HD]
    high = own[:, HD:] + came[:, HD:]
    first = where[0] == 0
    out_ref[...] = jnp.where(first, low, high)
    send_ref[...] = jnp.where(first, high, low).astype(send_ref.dtype)


def half_sum_kernel(where, own, came, out_ref):
    out_ref[...] = (own[...] + came[...]).astype(out_ref.dtype)


def pair_kernel(where, one, two, resid, out_ref):
    low = one[:, :HD].astype(jnp.float32) + two[:, :HD].astype(jnp.float32)
    high = one[:, HD:].astype(jnp.float32) + two[:, HD:].astype(jnp.float32)
    first = where[0] == 0
    own, other = jnp.where(first, low, high), jnp.where(first, high, low)
    out_ref[:ROWS, :] = (resid[:ROWS, :].astype(jnp.float32) + own).astype(jnp.bfloat16)
    out_ref[ROWS:, :] = (resid[ROWS:, :].astype(jnp.float32) + other).astype(jnp.bfloat16)


def mix(where, attn, weights):
    with jax.named_scope("gather_attn"):
        blocks = along_z_all(attn)
    with jax.named_scope("mix"):
        early = call(
            mix_early,
            jax.ShapeDtypeStruct((ROWS, 512), jnp.float32),
            where,
            *blocks[:4],
            weights,
            flops=2 * ROWS * 512 * 512,
            moved=2**21,
        )
        pair = jax.ShapeDtypeStruct((ROWS, 2 * HD), jnp.float32)
        own, send = call(
            mix_late,
            (pair, pair),
            where,
            *blocks[4:],
            early,
            weights,
            flops=2 * ROWS * 512 * 512,
            moved=2**21,
        )
        return own, to_other_core(send)


def mix_to_pair(where, attn, weights, resid):
    sums = mix(where, attn, weights)
    with jax.named_scope("mix"):
        halves = jax.ShapeDtypeStruct((ROWS, 2 * HD), jnp.bfloat16)
        one = call(half_sum_kernel, halves, where, *sums, moved=2**20)
        pair = jax.ShapeDtypeStruct((2 * ROWS, HD), jnp.bfloat16)
        return call(pair_kernel, pair, where, one, over_x(one), resid, moved=2**20)


def mix_to_own(where, attn, weights, resid):
    sums = mix(where, attn, weights)
    with jax.named_scope("mix"):
        own, send = call(
            split_kernel,
            (
                jax.ShapeDtypeStruct((ROWS, HD), jnp.float32),
                jax.ShapeDtypeStruct((ROWS, HD), jnp.bfloat16),
            ),
            where,
            *sums,
            moved=2**20,
        )
        summed = own + over_x(send).astype(jnp.float32)
        return (resid.astype(jnp.float32) + summed).astype(jnp.bfloat16)


def column_part(out_one, out_two, index):
    with jax.named_scope("columns"):
        parts = [
            lax.dynamic_slice_in_dim(out, index * 16, 16, axis=0).reshape(16, 2, Z, 256)
            for out in (out_one, out_two)
        ]
        part = jnp.transpose(jnp.stack(parts), (3, 0, 1, 2, 4)).reshape(Z, 32, 512)
        groups = [[xh * 16 + z * 2 + c for z in range(Z)] for xh in range(2) for c in range(2)]
        return lax.all_to_all(part, "head", 0, 0, axis_index_groups=groups, tiled=True)


def column_rows(part):
    with jax.named_scope("columns"):
        return lax.all_gather(part, "ctx", axis=1, tiled=True).reshape(1024, 512)


def local(tokens, lengths, gain_one, qkv_one, out_one, gain_two, qkv_two, out_two):
    index = lax.axis_index("ctx").astype(jnp.int32)
    head = lax.axis_index("head").astype(jnp.int32)
    c = head % 2
    at = jnp.where(jnp.arange(6) < 3, head, index)
    where = jnp.right_shift(at, np.array([4, 1, 0, 2, 0, 0])) & np.array([1, 7, 1, 1, 3, 7])

    planes_one = jnp.transpose(qkv_one, (1, 0, 2))
    planes_two = jnp.transpose(qkv_two, (1, 0, 2))
    with jax.named_scope("swap"):
        others_one = to_other_core(planes_one)
    with jax.named_scope("gather_tokens"):
        part = column_part(out_one, out_two, index)
        tokens_pair = jnp.concatenate([tokens, over_x(tokens)], axis=0)
        part_one, part_two = part[:, :16], part[:, 16:]
        tokens_pair = after(tokens_pair, part_one, part_two)
        columns_one = column_rows(part_one)
        blocks = along_z_all(tokens_pair)
    query, kv = project(where, blocks, gain_one, planes_one, others_one)
    half = jax.ShapeDtypeStruct((ROWS, HD), jnp.bfloat16)
    with jax.named_scope("within"):
        kv = after(kv, columns_one)
        prev = lax.ppermute(kv, "ctx", [(i, i + 1) for i in range(7)])
        others_two = to_other_core(after(planes_two, kv))
        attn = call(
            within_kernel, half, where, lengths, query, kv, prev, flops=2**28, moved=2**20, scalars=2
        )
    pair = mix_to_pair(where, attn, columns_one, tokens_pair)

    with jax.named_scope("gather_stream"):
        pair = after(pair, others_two)
        columns_two = column_rows(after(part_two, pair))
        blocks = along_z_all(pair)
    query, kv = project(where, blocks, gain_two, planes_two, others_two)
    attn = after(across(where, query, kv), columns_two)
    return mix_to_own(where, attn, columns_two, pair[:ROWS])


def solution(mesh):
    placed = (
        P("ctx", "head"),
        P(),
        P(),
        P(None, None, "head"),
        P("head", None),
        P(),
        P(None, None, "head"),
        P("head", None),
    )
    return jax.shard_map(
        local, mesh=mesh, in_specs=placed, out_specs=P("ctx", "head"), check_vma=False
    )
```

```python
import jax
import jax.numpy as jnp
import numpy as np
from jax import lax
from jax.experimental import pallas as pl
from jax.experimental.pallas import tpu as pltpu
from jax.sharding import PartitionSpec as P

HD = 128
EPS = 1e-05
D = 4096
ROWS = 512
Z = 8
SCALE = HD ** (-0.5) * 1.4426950408889634
STEPS = (0, -1, 1, -2, 2, -3, 3, 4)
ANYWHERE = pl.BlockSpec(memory_space=pltpu.VMEM)
SCALARS = pl.BlockSpec(memory_space=pltpu.SMEM)


def call(kernel, out, *args, flops=0, moved=0, scratch=(), scalars=1, limit=12):
    return pl.pallas_call(
        kernel,
        out_shape=out,
        in_specs=[SCALARS] * scalars + [ANYWHERE] * (len(args) - scalars),
        out_specs=jax.tree.map(lambda _: ANYWHERE, out),
        scratch_shapes=list(scratch),
        compiler_params=pltpu.CompilerParams(vmem_limit_bytes=limit * 2**20),
        cost_estimate=pl.CostEstimate(flops=flops, bytes_accessed=moved, transcendentals=0),
    )(*args)


def head_perm(dxh=0, dz=0, dc=0):
    pairs = []
    for xh in range(2):
        for z in range(Z):
            for c in range(2):
                to = ((xh + dxh) % 2) * 16 + ((z + dz) % Z) * 2 + (c + dc) % 2
                pairs.append((xh * 16 + z * 2 + c, to))
    return pairs


def ctx_perm(dxl=0, dy=0):
    return [
        (xl * 4 + y, ((xl + dxl) % 2) * 4 + (y + dy) % 4) for xl in range(2) for y in range(4)
    ]


def along_z(value, steps):
    return lax.ppermute(value, "head", head_perm(dz=steps))


def to_other_core(value):
    return lax.ppermute(value, "head", head_perm(dc=1))


def along_z_all(block, *due):
    half = block.shape[0] // 2
    f1, b1 = (along_z(block, k) for k in (1, -1))
    f2, b2 = (along_z(after(block, *due) if due else block, k) for k in (2, -2))
    f3, b3 = along_z(f2, 1), along_z(b2, -1)
    g1, g2 = along_z(f2[:half], 2), along_z(b2[half:], -2)
    return (block, f1, b1, f2, b2, f3, b3, g1, g2)


def over_x(value):
    return lax.ppermute(value, "head", head_perm(dxh=1))


def after(value, *others):
    return lax.optimization_barrier((value, others))[0]


def product(where, parts, gain, mine, others):
    xh, z, c = where[0], where[1], where[2]
    acc = jnp.zeros((ROWS, 768), jnp.float32)
    squares = jnp.zeros((ROWS, HD), jnp.float32)
    for step, one, two in parts:
        at = jnp.bitwise_and(z + step, Z - 1)
        scaled, weights = [], []
        for rows, x in ((one, xh), (two, 1 - xh)):
            wide = rows.astype(jnp.float32)
            squares += wide * wide
            head = (x * Z + at) * 2 + c
            scaled.append((wide * gain[pl.ds(head, 1), :]).astype(jnp.bfloat16))
            first = pl.multiple_of(head * HD, HD)
            weights.append(
                jnp.concatenate(
                    [mine[t, pl.ds(first, HD), :] for t in range(3)]
                    + [others[t, pl.ds(first, HD), :] for t in range(3)],
                    axis=1,
                )
            )
        acc += jnp.dot(
            jnp.concatenate(scaled, axis=1),
            jnp.concatenate(weights, axis=0),
            preferred_element_type=jnp.float32,
        )
    return acc, squares


def project_early(where, *refs):
    blocks, (gain, mine, others, acc_ref, squares_ref) = refs[:5], refs[5:]
    parts = [(k, ref[:ROWS, :], ref[ROWS:, :]) for k, ref in zip(STEPS, blocks)]
    acc_ref[...], squares_ref[...] = product(where, parts, gain, mine, others)


def project_late(where, *refs):
    blocks, (acc_early, squares_early, gain, mine, others, out_ref, send_ref) = refs[:4], refs[4:]
    parts = [(k, ref[:ROWS, :], ref[ROWS:, :]) for k, ref in zip(STEPS[5:], blocks[:2])]
    parts.append((STEPS[7], blocks[2][...], blocks[3][...]))
    acc, squares = product(where, parts, gain, mine, others)
    acc += acc_early[...]
    squares += squares_early[...]
    total = jnp.broadcast_to(jnp.sum(squares, axis=1, keepdims=True), (ROWS, HD))
    out_ref[:, :384] = acc[:, :384]
    out_ref[:, 384:] = total
    send_ref[:, :384] = acc[:, 384:]
    send_ref[:, 384:] = total


def finish_kernel(where, own, came, q_ref, kv_ref):
    total = own[:, 384:] + came[:, 384:]
    factor = lax.rsqrt(total * (1.0 / D) + EPS)
    q_ref[...] = ((own[:, :128] + came[:, :128]) * factor).astype(jnp.bfloat16)
    kv_ref[:, :128] = ((own[:, 128:256] + came[:, 128:256]) * factor).astype(jnp.bfloat16)
    kv_ref[:, 128:] = ((own[:, 256:384] + came[:, 256:384]) * factor).astype(jnp.bfloat16)


def project(where, blocks, gain, mine, others):
    with jax.named_scope("project"):
        gain = gain.reshape(32, HD)
        early = call(
            project_early,
            (
                jax.ShapeDtypeStruct((ROWS, 768), jnp.float32),
                jax.ShapeDtypeStruct((ROWS, HD), jnp.float32),
            ),
            where,
            *blocks[:5],
            gain,
            mine,
            others,
            flops=2 * ROWS * 1280 * 768,
            moved=6 * 2**20,
        )
        wide = jax.ShapeDtypeStruct((ROWS, 512), jnp.float32)
        own, send = call(
            project_late,
            (wide, wide),
            where,
            *blocks[5:],
            *early,
            gain,
            mine,
            others,
            flops=2 * ROWS * 768 * 768,
            moved=6 * 2**20,
        )
        came = to_other_core(send)
        return call(
            finish_kernel,
            (
                jax.ShapeDtypeStruct((ROWS, HD), jnp.bfloat16),
                jax.ShapeDtypeStruct((ROWS, 2 * HD), jnp.bfloat16),
            ),
            where,
            own,
            came,
            moved=3 * 2**20,
        )


def scores_of(query, keys):
    return (
        lax.dot_general(query, keys, (((1,), (1,)), ((), ())), preferred_element_type=jnp.float32)
        * SCALE
    )


def within_kernel(where, lengths, q_ref, kv_ref, prev_ref, out_ref):
    query = q_ref[...]
    first = where[5] * ROWS
    place = lax.broadcasted_iota(jnp.int32, (8, ROWS), 1) + first
    start = jnp.zeros((8, ROWS), jnp.int32)
    end = jnp.int32(0)
    for s in range(lengths.shape[0]):
        end = end + lengths[s]
        start = jnp.where(end <= place, end, start)
    start = jnp.broadcast_to(start[:1, :].astype(jnp.float32), (HD, ROWS))
    start = jnp.transpose(start)[:, :1].astype(jnp.int32)
    row = lax.broadcasted_iota(jnp.int32, (ROWS, ROWS), 0) + first
    col = lax.broadcasted_iota(jnp.int32, (ROWS, ROWS), 1) + first
    ok_own = (col <= row) & (col >= start)
    ok_prev = (col - ROWS) >= start
    s_own = jnp.where(ok_own, scores_of(query, kv_ref[:, :HD]), -1e30)
    s_prev = jnp.where(ok_prev, scores_of(query, prev_ref[:, :HD]), -1e30)
    top = jnp.maximum(
        jnp.max(s_own, axis=1, keepdims=True), jnp.max(s_prev, axis=1, keepdims=True)
    )
    e_own = jnp.exp2(s_own - top)
    e_prev = jnp.exp2(s_prev - top)
    total = jnp.sum(e_own, axis=1, keepdims=True) + jnp.sum(e_prev, axis=1, keepdims=True)
    mixed = jnp.dot(
        e_own.astype(jnp.bfloat16), kv_ref[:, HD:], preferred_element_type=jnp.float32
    ) + jnp.dot(e_prev.astype(jnp.bfloat16), prev_ref[:, HD:], preferred_element_type=jnp.float32)
    out_ref[...] = (mixed / total).astype(jnp.bfloat16)


def start_state(query, keys, values, state):
    s = scores_of(query, keys)
    row = lax.broadcasted_iota(jnp.int32, (ROWS, ROWS), 0)
    col = lax.broadcasted_iota(jnp.int32, (ROWS, ROWS), 1)
    s = jnp.where(col <= row, s, -1e30)
    top = jnp.max(s, axis=1, keepdims=True)
    expo = jnp.exp2(s - top)
    state[0][...] = top
    state[1][...] = jnp.sum(expo, axis=1, keepdims=True)
    state[2][...] = jnp.dot(expo.astype(jnp.bfloat16), values, preferred_element_type=jnp.float32)


def add_keys(query, keys, values, state):
    s = scores_of(query, keys)
    old = state[0][...]
    top = jnp.maximum(old, jnp.max(s, axis=1, keepdims=True))
    expo = jnp.exp2(s - top)
    shrink = jnp.exp2(old - top)
    state[0][...] = top
    state[1][...] = state[1][...] * shrink + jnp.sum(expo, axis=1, keepdims=True)
    state[2][...] = state[2][...] * shrink + jnp.dot(
        expo.astype(jnp.bfloat16), values, preferred_element_type=jnp.float32
    )


STATE = (
    pltpu.VMEM((ROWS, 1), jnp.float32),
    pltpu.VMEM((ROWS, 1), jnp.float32),
    pltpu.VMEM((ROWS, HD), jnp.float32),
)
STATS = jax.ShapeDtypeStruct((8, ROWS), jnp.float32)


def give(state, out_ref, stat_ref):
    total = state[1][...]
    out_ref[...] = (state[2][...] / total).astype(out_ref.dtype)
    lane = lax.broadcasted_iota(jnp.int32, (ROWS, HD), 1)
    both = jnp.where(lane == 0, state[0][...], total)
    stat_ref[...] = jnp.transpose(both)[:8, :]


def helped_kernel(where, q_ref, kv0, kv1, kv2, kv3, out_ref, stat_ref, *state):
    @pl.when(where[3] == 0)
    def _():
        query = q_ref[...]
        state[0][...] = jnp.full((ROWS, 1), -1e30, jnp.float32)
        state[1][...] = jnp.zeros((ROWS, 1), jnp.float32)
        state[2][...] = jnp.zeros((ROWS, HD), jnp.float32)
        for ref in (kv0, kv1, kv2, kv3):
            add_keys(query, ref[:, :HD], ref[:, HD:], state)
        give(state, out_ref, stat_ref)

    @pl.when(where[3] != 0)
    def _():
        out_ref[...] = jnp.zeros((ROWS, HD), out_ref.dtype)
        stat_ref[...] = jnp.zeros((8, ROWS), jnp.float32)


def across_kernel(where, q_ref, kv0, kv1, kv2, kv3, out_ref, stat_ref, *state):
    y = where[4]
    query = q_ref[...]
    start_state(query, kv0[:, :HD], kv0[:, HD:], state)
    for ref, dy in ((kv1, -1), (kv2, 1), (kv3, 2)):

        @pl.when(jnp.bitwise_and(y + dy, 3) < y)
        def _(ref=ref):
            add_keys(query, ref[:, :HD], ref[:, HD:], state)

    give(state, out_ref, stat_ref)


def merge_kernel(where, one, stat_one, two, stat_two, out_ref):
    a, b = stat_one[...], stat_two[...]
    second = where[3] != 0
    top_a, total_a = a[0:1, :], a[1:2, :]
    top_b = jnp.where(second, b[0:1, :], -1e30)
    total_b = jnp.where(second, b[1:2, :], 0.0)
    top = jnp.maximum(top_a, top_b)
    share_a = total_a * jnp.exp2(top_a - top)
    share_b = total_b * jnp.exp2(top_b - top)
    part = share_b / (share_a + share_b)
    part = jnp.transpose(jnp.broadcast_to(part, (HD, ROWS)))
    first = one[...]
    out_ref[...] = (first + (two[...].astype(jnp.float32) - first) * part).astype(jnp.bfloat16)


def across(where, query, kv):
    with jax.named_scope("across"):
        half = jax.ShapeDtypeStruct((ROWS, HD), jnp.bfloat16)
        full = jax.ShapeDtypeStruct((ROWS, HD), jnp.float32)
        sent = [lax.ppermute(kv, "ctx", ctx_perm(dy=k)) for k in (1, -1, 2)]
        asked = lax.ppermute(query, "ctx", [(4 + y, y) for y in range(4)])
        args = (kv, *sent)
        helped, helped_stat = call(
            helped_kernel, (half, STATS), where, asked, *args, flops=2**30, moved=2**22, scratch=STATE
        )
        back = [(y, 4 + y) for y in range(4)]
        two, two_stat = (lax.ppermute(v, "ctx", back) for v in (helped, helped_stat))
        one, one_stat = call(
            across_kernel, (full, STATS), where, query, *args, flops=2**30, moved=2**22, scratch=STATE
        )
        return call(merge_kernel, half, where, one, one_stat, two, two_stat, moved=2**20)


def mixed(where, rows, steps, weights):
    z = where[1]
    acc = jnp.zeros((ROWS, 512), jnp.float32)
    for k in range(0, len(steps), 2):
        features = [
            weights[pl.ds(pl.multiple_of(jnp.bitwise_and(z + step, Z - 1) * HD, HD), HD), :]
            for step in steps[k : k + 2]
        ]
        acc += jnp.dot(
            jnp.concatenate(rows[k : k + 2], axis=1),
            jnp.concatenate(features, axis=0),
            preferred_element_type=jnp.float32,
        )
    return acc


def mix_early(where, r0, r1, r2, r3, weights, acc_ref):
    rows = [ref[...] for ref in (r0, r1, r2, r3)]
    acc_ref[...] = mixed(where, rows, STEPS[:4], weights)


def mix_late(where, r4, r5, r6, low, high, early, weights, out_ref, send_ref):
    rows = [ref[...] for ref in (r4, r5, r6)]
    rows.append(jnp.concatenate([low[...], high[...]], axis=0))
    acc = early[...] + mixed(where, rows, STEPS[4:], weights)
    first = where[2] == 0
    for x in range(2):
        at = x * HD
        low, high = acc[:, 2 * at : 2 * at + HD], acc[:, 2 * at + HD : 2 * at + 2 * HD]
        out_ref[:, at : at + HD] = jnp.where(first, low, high)
        send_ref[:, at : at + HD] = jnp.where(first, high, low)


def split_kernel(where, own, came, out_ref, send_ref):
    low = own[:, :HD] + came[:, :HD]
    high = own[:, HD:] + came[:, HD:]
    first = where[0] == 0
    out_ref[...] = jnp.where(first, low, high)
    send_ref[...] = jnp.where(first, high, low).astype(send_ref.dtype)


def half_sum_kernel(where, own, came, out_ref):
    out_ref[...] = (own[...] + came[...]).astype(out_ref.dtype)


def pair_kernel(where, one, two, resid, out_ref):
    low = one[:, :HD].astype(jnp.float32) + two[:, :HD].astype(jnp.float32)
    high = one[:, HD:].astype(jnp.float32) + two[:, HD:].astype(jnp.float32)
    first = where[0] == 0
    own, other = jnp.where(first, low, high), jnp.where(first, high, low)
    out_ref[:ROWS, :] = (resid[:ROWS, :].astype(jnp.float32) + own).astype(jnp.bfloat16)
    out_ref[ROWS:, :] = (resid[ROWS:, :].astype(jnp.float32) + other).astype(jnp.bfloat16)


def mix(where, attn, weights):
    with jax.named_scope("gather_attn"):
        blocks = along_z_all(attn)
    with jax.named_scope("mix"):
        early = call(
            mix_early,
            jax.ShapeDtypeStruct((ROWS, 512), jnp.float32),
            where,
            *blocks[:4],
            weights,
            flops=2 * ROWS * 512 * 512,
            moved=2**21,
        )
        pair = jax.ShapeDtypeStruct((ROWS, 2 * HD), jnp.float32)
        own, send = call(
            mix_late,
            (pair, pair),
            where,
            *blocks[4:],
            early,
            weights,
            flops=2 * ROWS * 512 * 512,
            moved=2**21,
        )
        return own, to_other_core(send)


def mix_to_pair(where, attn, weights, resid, due):
    sums = mix(where, attn, weights)
    with jax.named_scope("mix"):
        halves = jax.ShapeDtypeStruct((ROWS, 2 * HD), jnp.bfloat16)
        one = after(call(half_sum_kernel, halves, where, *sums, moved=2**20), due)
        pair = jax.ShapeDtypeStruct((2 * ROWS, HD), jnp.bfloat16)
        return call(pair_kernel, pair, where, one, over_x(one), resid, moved=2**20)


def mix_to_own(where, attn, weights, resid):
    sums = mix(where, attn, weights)
    with jax.named_scope("mix"):
        own, send = call(
            split_kernel,
            (
                jax.ShapeDtypeStruct((ROWS, HD), jnp.float32),
                jax.ShapeDtypeStruct((ROWS, HD), jnp.bfloat16),
            ),
            where,
            *sums,
            moved=2**20,
        )
        summed = own + over_x(send).astype(jnp.float32)
        return (resid.astype(jnp.float32) + summed).astype(jnp.bfloat16)


def column_part(out_one, out_two, index):
    with jax.named_scope("columns"):
        parts = [
            lax.dynamic_slice_in_dim(out, index * 16, 16, axis=0).reshape(16, 2, Z, 256)
            for out in (out_one, out_two)
        ]
        part = jnp.transpose(jnp.stack(parts), (3, 0, 1, 2, 4)).reshape(Z, 32, 512)
        groups = [[xh * 16 + z * 2 + c for z in range(Z)] for xh in range(2) for c in range(2)]
        return lax.all_to_all(part, "head", 0, 0, axis_index_groups=groups, tiled=True)


def column_rows(part):
    with jax.named_scope("columns"):
        return lax.all_gather(part, "ctx", axis=1, tiled=True).reshape(1024, 512)


def local(tokens, lengths, gain_one, qkv_one, out_one, gain_two, qkv_two, out_two):
    index = lax.axis_index("ctx").astype(jnp.int32)
    head = lax.axis_index("head").astype(jnp.int32)
    c = head % 2
    at = jnp.where(jnp.arange(6) < 3, head, index)
    where = jnp.right_shift(at, np.array([4, 1, 0, 2, 0, 0])) & np.array([1, 7, 1, 1, 3, 7])

    planes_one = jnp.transpose(qkv_one, (1, 0, 2))
    planes_two = jnp.transpose(qkv_two, (1, 0, 2))
    with jax.named_scope("swap"):
        others_one = to_other_core(planes_one)
    with jax.named_scope("gather_tokens"):
        tokens_pair = jnp.concatenate([tokens, over_x(tokens)], axis=0)
        part = column_part(out_one, out_two, index)
        part = after(part, tokens_pair)
        part_one, part_two = part[:, :16], part[:, 16:]
        columns_one = column_rows(part_one)
        blocks = along_z_all(tokens_pair, part_one, part_two)
    query, kv = project(where, blocks, gain_one, planes_one, others_one)
    half = jax.ShapeDtypeStruct((ROWS, HD), jnp.bfloat16)
    with jax.named_scope("within"):
        kv = after(kv, columns_one)
        columns_two = column_rows(after(part_two, columns_one))
        prev = lax.ppermute(kv, "ctx", [(i, i + 1) for i in range(7)])
        others_two = to_other_core(after(planes_two, kv))
        attn = call(
            within_kernel, half, where, lengths, query, kv, prev, flops=2**28, moved=2**20, scalars=2
        )
    pair = mix_to_pair(where, attn, columns_one, tokens_pair, columns_two)

    with jax.named_scope("gather_stream"):
        pair = after(pair, others_two)
        blocks = along_z_all(pair)
    query, kv = project(where, blocks, gain_two, planes_two, others_two)
    attn = across(where, query, kv)
    return mix_to_own(where, attn, columns_two, pair[:ROWS])


def solution(mesh):
    placed = (
        P("ctx", "head"),
        P(),
        P(),
        P(None, None, "head"),
        P("head", None),
        P(),
        P(None, None, "head"),
        P("head", None),
    )
    return jax.shard_map(
        local, mesh=mesh, in_specs=placed, out_specs=P("ctx", "head"), check_vma=False
    )
```
